32 devices in a mesh: dp: 4 (over z), ctx: 8 (over y, x, core).
Axes of the slice: x: 2, y: 2, z: 4, core: 2. Of those that a mesh axis runs over, the one named last changes fastest.
Arguments:
- queries: bfloat16 [4096, 4096], P(('dp', 'ctx')), parts along dimension 0, may hold values from -0.6640625 to 0.6640625
- key_vectors: bfloat16 [4096, 4096], P(('dp', 'ctx')), parts along dimension 0, may hold values from -0.6640625 to 0.6640625
- values: bfloat16 [4096, 4096], P(('dp', 'ctx')), parts along dimension 0, may hold values from -0.6640625 to 0.6640625
- out_grad: bfloat16 [4096, 4096], P(('dp', 'ctx')), parts along dimension 0, may hold values from -0.6640625 to 0.6640625
- log_decay: bfloat16 [4096, 32], P(('dp', 'ctx')), parts along dimension 0, may hold values from -2.2 to 0
Outputs:
- attended: bfloat16 [4096, 4096], P(('dp', 'ctx')), parts along dimension 0
- query_grad: bfloat16 [4096, 4096], P(('dp', 'ctx')), parts along dimension 0
- key_grad: bfloat16 [4096, 4096], P(('dp', 'ctx')), parts along dimension 0
- value_grad: bfloat16 [4096, 4096], P(('dp', 'ctx')), parts along dimension 0
The draws below stay inside these ranges and needn't reach their ends.
There are 4 independent parts, one for each index of `dp`. The reference program is written for one: setup_inputs(seed, part) draws one part's arguments, and reference() takes and returns one part's arrays. A program takes and returns all parts, laid end to end along the dimension named above; each array names one. Nothing has to cross between parts.
All inputs are finite; a program needn't handle non-finite values.
Results may differ from the reference program's by a relative error of at most 0.001.
Values may be sent and summed in bfloat16 or wider, within the bound.
A program may use at most 320 MiB of HBM per device.

```python
import math
import jax
import jax.numpy as jnp
from jax import lax

HEAD_COUNT_HALF = 32
DK = 128
SPAN = 64
TOK_DEV = 128
TOKEN_LENGTH = 1024


def draw_log_decay(key, part):
    key_rows_full = jax.random.split(key, 8)
    keep_share = 5
    slow_heads = jax.random.randint(key_rows_full[0], (HEAD_COUNT_HALF,), 0, 10) < keep_share
    fast_rate = jnp.exp(jax.random.uniform(key_rows_full[1], (HEAD_COUNT_HALF,), jnp.float32, math.log(1.0 / 50.0), math.log(1.0 / 30.0)))
    slow_rate = jnp.exp(jax.random.uniform(key_rows_full[2], (HEAD_COUNT_HALF,), jnp.float32, math.log(0.02 / TOKEN_LENGTH), math.log(0.5 / TOKEN_LENGTH)))
    per_head_rate = jnp.where(slow_heads, slow_rate, fast_rate)
    random_noise = jax.random.uniform(key_rows_full[3], (TOKEN_LENGTH, HEAD_COUNT_HALF), jnp.float32, 0.5, 2.0)
    token_positions = jnp.arange(TOKEN_LENGTH)
    segment_shift = jax.random.randint(key_rows_full[6], (), 0, TOK_DEV)
    segment_index = (token_positions + segment_shift) // TOK_DEV
    segment_count = TOKEN_LENGTH // TOK_DEV + 1
    segment_scale = jnp.exp(jax.random.uniform(key_rows_full[7], (segment_count, HEAD_COUNT_HALF), jnp.float32, math.log(0.01), 0.0))
    segment_factor = segment_scale[segment_index]
    spike_locations = jax.random.randint(key_rows_full[4], (3,), 0, TOKEN_LENGTH)
    spike_depth = jax.random.uniform(key_rows_full[5], (3, HEAD_COUNT_HALF), jnp.float32, math.log(0.5), math.log(0.8))
    spike_hits = (token_positions[None, :, None] == spike_locations[:, None, None]).astype(jnp.float32)
    spike_events = jnp.sum(spike_hits * spike_depth[:, None, :], axis=0)
    return (-per_head_rate[None, :] * random_noise * segment_factor + spike_events).astype(jnp.bfloat16)


def levels(key, dims, cuts, low, top_value):
    def one(dim, blocks):
        draws = jax.random.uniform(jax.random.fold_in(jax.random.fold_in(key, 6), dim), (blocks,), jnp.float32, low / len(cuts), top_value / len(cuts))
        return jnp.repeat(jnp.exp(draws), dims[dim] // blocks).reshape((-1,) + (1,) * (len(dims) - dim - 1))

    level = one(*cuts[0])
    for cut in cuts[1:]:
        level = level * one(*cut)
    return level


def centred(key, shape, scale, most, cuts=(), kind=jnp.bfloat16):
    values = jax.random.normal(key, shape, jnp.float32) * scale
    if len(cuts) > 0:
        values = levels(key, shape, cuts, -0.22, 0.18) * values
    return jnp.clip(values, min=-most, max=most).astype(kind)


def setup_inputs(seed: int = 0, part: int = 0) -> dict:
    arg_keys = jax.random.split(jax.random.key(seed), 6)
    part_splits = jax.random.split(jax.random.fold_in(arg_keys[5], part), 6)
    queries = centred(part_splits[0], (TOKEN_LENGTH, HEAD_COUNT_HALF * DK), 0.111, 0.6640625, ((0, 8),))
    key_vectors = centred(part_splits[1], (TOKEN_LENGTH, HEAD_COUNT_HALF * DK), 0.111, 0.6640625, ((0, 8),))
    values = centred(part_splits[2], (TOKEN_LENGTH, HEAD_COUNT_HALF * DK), 0.111, 0.6640625, ((0, 8),))
    out_grad = centred(part_splits[3], (TOKEN_LENGTH, HEAD_COUNT_HALF * DK), 0.111, 0.6640625, ((0, 8),))
    log_decay = draw_log_decay(jax.random.fold_in(jax.random.fold_in(arg_keys[5], part), 71), part)
    return {"queries": queries, "key_vectors": key_vectors, "values": values, "out_grad": out_grad, "log_decay": log_decay}


def combine(earlier, latter):
    return (earlier[0] + latter[0], jnp.exp(latter[0])[..., None, None] * earlier[1] + latter[1])


def head_pass(queries, key_vectors, values, out_grad, log_decay, state_in, grad_in):
    highest = lax.Precision.HIGHEST
    blocks = queries.shape[0] // SPAN
    q_rows = queries.reshape(blocks, SPAN, -1)
    k_rows = key_vectors.reshape(blocks, SPAN, -1)
    v_rows = values.reshape(blocks, SPAN, -1)
    g_rows = out_grad.reshape(blocks, SPAN, -1)
    cumul = jnp.cumsum(log_decay.reshape(blocks, SPAN), axis=1)
    totals = cumul[:, -1]
    causal = jnp.tril(jnp.ones((SPAN, SPAN), dtype=bool))
    spread = cumul[:, :, None] - cumul[:, None, :]
    weights = jnp.where(causal, jnp.exp(jnp.where(causal, spread, 0.0)), 0.0)
    scores = jnp.einsum("nte,nse->nts", q_rows, k_rows, precision=highest) * weights
    grad_scores = jnp.einsum("nte,nse->nts", g_rows, v_rows, precision=highest) * weights
    key_decay = jnp.exp(totals[:, None] - cumul)[:, :, None]
    query_decay = jnp.exp(cumul)[:, :, None]
    q_scaled = q_rows * query_decay
    g_scaled = g_rows * query_decay
    k_scaled = k_rows * key_decay
    v_scaled = v_rows * key_decay
    updates = jnp.einsum("nse,nsf->nef", k_scaled, v_rows, precision=highest)
    grad_states = jnp.einsum("nte,ntf->nef", q_scaled, g_rows, precision=highest)
    anchor = jnp.zeros((1,), jnp.float32)
    forward = lax.associative_scan(combine, (jnp.concatenate([anchor, totals]), jnp.concatenate([state_in[None], updates])))
    starts = forward[1][:blocks]
    backward = lax.associative_scan(combine, (jnp.concatenate([anchor, totals[::-1]]), jnp.concatenate([grad_in[None], grad_states[::-1]])))
    after_grad = backward[1][:blocks][::-1]
    attended = jnp.einsum("nte,nef->ntf", q_scaled, starts, precision=highest) + jnp.einsum("nts,nsf->ntf", scores, v_rows, precision=highest)
    query_grad = jnp.einsum("ntf,nef->nte", g_scaled, starts, precision=highest) + jnp.einsum("nts,nse->nte", grad_scores, k_rows, precision=highest)
    key_grad = jnp.einsum("nsf,nef->nse", v_scaled, after_grad, precision=highest) + jnp.einsum("nts,nte->nse", grad_scores, q_rows, precision=highest)
    value_grad = jnp.einsum("nse,nef->nsf", k_scaled, after_grad, precision=highest) + jnp.einsum("nts,ntf->nsf", scores, g_rows, precision=highest)
    length = queries.shape[0]
    return (attended.reshape(length, -1), query_grad.reshape(length, -1), key_grad.reshape(length, -1), value_grad.reshape(length, -1))


def split_heads(matrix, head_count):
    return jnp.transpose(matrix.reshape(matrix.shape[0], head_count, -1), (1, 0, 2)).astype(jnp.float32)


def join_heads(stacked):
    return jnp.transpose(stacked, (1, 0, 2)).reshape(stacked.shape[1], -1).astype(jnp.bfloat16)


def run_head(pieces):
    return head_pass(*pieces)


def reference(queries, key_vectors, values, out_grad, log_decay):
    empty_state = jnp.zeros((HEAD_COUNT_HALF, DK, DK), jnp.float32)
    decays = jnp.transpose(log_decay).astype(jnp.float32)
    results = lax.map(run_head, (split_heads(queries, HEAD_COUNT_HALF), split_heads(key_vectors, HEAD_COUNT_HALF), split_heads(values, HEAD_COUNT_HALF), split_heads(out_grad, HEAD_COUNT_HALF), decays, empty_state, empty_state))
    return (join_heads(results[0]), join_heads(results[1]), join_heads(results[2]), join_heads(results[3]))
```

```python
import functools

import jax
import jax.numpy as jnp
from jax import lax
from jax.experimental import pallas as pl
from jax.experimental.pallas import tpu as pltpu
from jax.sharding import PartitionSpec as P

MESH = pl.DeviceIdType.MESH
HEADS_PER_CHUNK = 2


def mm(a, b, ca, cb):
    return lax.dot_general(
        a, b, (((ca,), (cb,)), ((), ())), preferred_element_type=jnp.float32
    )


def split(x):
    high = x.astype(jnp.bfloat16)
    return high, (x - high.astype(jnp.float32)).astype(jnp.bfloat16)


def kernel(
    n, per, q_ref, k_ref, v_ref, g_ref, ld_ref, att_ref, dq_ref, dk_ref, dv_ref,
    fin, fout, bin_, bout, ecum, erest, etot, att0, dq0, dk0, dv0,
    fsend, frecv, bsend, brecv,
):
    me = lax.axis_index("ctx")
    up, down = lax.rem(me + 1, n), lax.rem(me + n - 1, n)
    tokens, heads = ld_ref.shape
    width = q_ref.shape[1] // heads
    chunks = heads // per
    bf16 = jnp.bfloat16

    barrier = pltpu.get_barrier_semaphore()

    @pl.when(me > 0)
    def _():
        pl.semaphore_signal(barrier, inc=1, device_id={"ctx": down}, device_id_type=MESH)

    @pl.when(me < n - 1)
    def _():
        pl.semaphore_signal(barrier, inc=1, device_id={"ctx": up}, device_id_type=MESH)

    pl.semaphore_wait(barrier, jnp.minimum(me, 1) + jnp.minimum(n - 1 - me, 1))

    @pl.when(me == 0)
    def _():
        fin[...] = jnp.zeros_like(fin)

    @pl.when(me == n - 1)
    def _():
        bin_[...] = jnp.zeros_like(bin_)

    row = lax.broadcasted_iota(jnp.int32, (tokens, tokens), 0)
    col = lax.broadcasted_iota(jnp.int32, (tokens, tokens), 1)
    causal = row >= col
    lower = jnp.where(causal, 1.0, 0.0).astype(bf16)
    upper = jnp.where(row < col, 1.0, 0.0).astype(bf16)
    head_row = lax.broadcasted_iota(jnp.int32, (heads, width), 0)

    def columns(h):
        return pl.ds(pl.multiple_of(h * width, width), width)

    def steps(h):
        pick = jnp.where(head_row == h, 1.0, 0.0).astype(bf16)
        return mm(ld_ref[...], pick, 1, 0)

    def forward_copy(c):
        part = pl.ds(c * per, per)
        return pltpu.make_async_remote_copy(
            src_ref=fout.at[part], dst_ref=fin.at[part],
            send_sem=fsend.at[c], recv_sem=frecv.at[c],
            device_id={"ctx": up}, device_id_type=MESH,
        )

    def backward_copy(c):
        part = pl.ds(c * per, per)
        return pltpu.make_async_remote_copy(
            src_ref=bout.at[part], dst_ref=bin_.at[part],
            send_sem=bsend.at[c], recv_sem=brecv.at[c],
            device_id={"ctx": down}, device_id_type=MESH,
        )

    def states(c):
        for j in range(per):
            h = c * per + j
            cols = columns(h)
            step = steps(h).astype(bf16)
            cum = mm(lower, step, 1, 0)
            ec = jnp.exp(cum)
            er = jnp.exp(mm(upper, step, 1, 0))
            ecum[h] = ec
            erest[h] = er
            etot[h] = jnp.broadcast_to(ec[tokens - 1 :, :], etot.shape[1:])
            kh, kl = split(k_ref[:, cols].astype(jnp.float32) * er)
            v = v_ref[:, cols]
            fout[h] = mm(kh, v, 0, 0) + mm(kl, v, 0, 0)
            qh, ql = split(q_ref[:, cols].astype(jnp.float32) * ec)
            g = g_ref[:, cols]
            bout[h] = mm(qh, g, 0, 0) + mm(ql, g, 0, 0)

    def forward(c):
        @pl.when(me > 0)
        def _():
            forward_copy(c).wait_recv()

        @pl.when(me < n - 1)
        def _():
            for j in range(per):
                h = c * per + j
                fout[h] = fout[h] + etot[h][:1, :] * fin[h]
            forward_copy(c).start()

    def backward(c):
        @pl.when(me < n - 1)
        def _():
            backward_copy(c).wait_recv()

        @pl.when(me > 0)
        def _():
            for j in range(per):
                h = c * per + j
                bout[h] = bout[h] + etot[h][:1, :] * bin_[h]
            backward_copy(c).start()

    def intra(c):
        for j in range(per):
            h = c * per + j
            cols = columns(h)
            q, k, v, g = q_ref[:, cols], k_ref[:, cols], v_ref[:, cols], g_ref[:, cols]
            between = jnp.where(row > col, steps(h), 0.0).astype(bf16)
            weights = jnp.where(causal, jnp.exp(mm(lower, between, 1, 0)), 0.0)
            sh, sl = split(mm(q, k, 1, 1) * weights)
            th, tl = split(mm(g, v, 1, 1) * weights)
            att0[:, cols] = mm(sh, v, 1, 0) + mm(sl, v, 1, 0)
            dq0[:, cols] = mm(th, k, 1, 0) + mm(tl, k, 1, 0)
            dk0[:, cols] = mm(th, q, 0, 0) + mm(tl, q, 0, 0)
            dv0[:, cols] = mm(sh, g, 0, 0) + mm(sl, g, 0, 0)

    def cross(c):
        for j in range(per):
            h = c * per + j
            cols = columns(h)
            q, k, v, g = q_ref[:, cols], k_ref[:, cols], v_ref[:, cols], g_ref[:, cols]
            ec, er = ecum[h], erest[h]
            ph, pl_ = split(fin[h])
            nh, nl = split(bin_[h])
            att_ref[:, cols] = (
                att0[:, cols] + ec * (mm(q, ph, 1, 0) + mm(q, pl_, 1, 0))
            ).astype(bf16)
            dq_ref[:, cols] = (
                dq0[:, cols] + ec * (mm(g, ph, 1, 1) + mm(g, pl_, 1, 1))
            ).astype(bf16)
            dk_ref[:, cols] = (
                dk0[:, cols] + er * (mm(v, nh, 1, 1) + mm(v, nl, 1, 1))
            ).astype(bf16)
            dv_ref[:, cols] = (
                dv0[:, cols] + er * (mm(k, nh, 1, 0) + mm(k, nl, 1, 0))
            ).astype(bf16)

    def guarded(c, work):
        @pl.when((c >= 0) & (c < chunks))
        def _():
            work(c)

    def tick(t, carry):
        guarded(t, states)
        guarded(t - me, forward)
        guarded(t - (n - 1 - me), backward)
        guarded(t, intra)
        guarded(t - jnp.maximum(me, n - 1 - me), cross)
        return carry

    lax.fori_loop(0, chunks + n - 1, tick, 0)

    def drain(c, carry):
        @pl.when(me < n - 1)
        def _():
            forward_copy(c).wait_send()

        @pl.when(me > 0)
        def _():
            backward_copy(c).wait_send()

        return carry

    lax.fori_loop(0, chunks, drain, 0)


def solution(mesh):
    n = mesh.shape["ctx"]

    def shards(queries, key_vectors, values, out_grad, log_decay):
        tokens, heads = log_decay.shape
        total = queries.shape[1]
        width = total // heads
        per = HEADS_PER_CHUNK
        chunks = heads // per
        f32 = jnp.float32
        vmem = pl.BlockSpec(memory_space=pltpu.VMEM)
        state = pltpu.VMEM((heads, width, width), f32)
        decay = pltpu.VMEM((heads, tokens, width), f32)
        rows = pltpu.VMEM((tokens, total), f32)
        sems = pltpu.SemaphoreType.DMA((chunks,))
        return pl.pallas_call(
            functools.partial(kernel, n, per),
            out_shape=[jax.ShapeDtypeStruct((tokens, total), jnp.bfloat16)] * 4,
            in_specs=[vmem] * 5,
            out_specs=[vmem] * 4,
            scratch_shapes=[state] * 4
            + [decay] * 2
            + [pltpu.VMEM((heads, 8, width), f32)]
            + [rows] * 4
            + [sems] * 4,
            compiler_params=pltpu.CompilerParams(
                collective_id=0, has_side_effects=True, vmem_limit_bytes=48 * 1024 * 1024
            ),
        )(queries, key_vectors, values, out_grad, log_decay)

    spec = P(("dp", "ctx"), None)
    return jax.shard_map(
        shards, mesh=mesh, in_specs=(spec,) * 5, out_specs=(spec,) * 4, check_vma=False
    )
```

```python
import functools

import jax
import jax.numpy as jnp
from jax import lax
from jax.experimental import pallas as pl
from jax.experimental.pallas import tpu as pltpu
from jax.sharding import PartitionSpec as P

MESH = pl.DeviceIdType.MESH
HEADS_PER_CHUNK = 2
LAG = 2


def mm(a, b, ca, cb):
    return lax.dot_general(
        a, b, (((ca,), (cb,)), ((), ())), preferred_element_type=jnp.float32
    )


def split(x):
    high = x.astype(jnp.bfloat16)
    return high, (x - high.astype(jnp.float32)).astype(jnp.bfloat16)


def pair(parts, axis):
    return jnp.concatenate(parts, axis=axis)


def kernel(
    n, per, q_ref, k_ref, v_ref, g_ref, ld_ref, att_ref, dq_ref, dk_ref, dv_ref,
    fin, fout, bin_, bout, ecum, erest, weights, etot, att0, dq0, dk0, dv0,
    fsend, frecv, bsend, brecv,
):
    me = lax.axis_index("ctx")
    up, down = lax.rem(me + 1, n), lax.rem(me + n - 1, n)
    tokens, heads = ld_ref.shape
    width = q_ref.shape[1] // heads
    chunks = heads // per
    bf16 = jnp.bfloat16

    barrier = pltpu.get_barrier_semaphore()

    @pl.when(me > 0)
    def _():
        pl.semaphore_signal(barrier, inc=1, device_id={"ctx": down}, device_id_type=MESH)

    @pl.when(me < n - 1)
    def _():
        pl.semaphore_signal(barrier, inc=1, device_id={"ctx": up}, device_id_type=MESH)

    pl.semaphore_wait(barrier, jnp.minimum(me, 1) + jnp.minimum(n - 1 - me, 1))

    row = lax.broadcasted_iota(jnp.int32, (tokens, tokens), 0)
    col = lax.broadcasted_iota(jnp.int32, (tokens, tokens), 1)
    causal = row >= col
    lower = jnp.where(causal, 1.0, 0.0).astype(bf16)
    upper = jnp.where(row < col, 1.0, 0.0).astype(bf16)
    head_row = lax.broadcasted_iota(jnp.int32, (heads, width), 0)

    def columns(h):
        return pl.ds(pl.multiple_of(h * width, width), width)

    def steps(h):
        pick = jnp.where(head_row == h, 1.0, 0.0).astype(bf16)
        return mm(ld_ref[...], pick, 1, 0)

    def forward_copy(c):
        part = pl.ds(c * per, per)
        return pltpu.make_async_remote_copy(
            src_ref=fout.at[part], dst_ref=fin.at[part],
            send_sem=fsend.at[c], recv_sem=frecv.at[c],
            device_id={"ctx": up}, device_id_type=MESH,
        )

    def backward_copy(c):
        part = pl.ds(c * per, per)
        return pltpu.make_async_remote_copy(
            src_ref=bout.at[part], dst_ref=bin_.at[part],
            send_sem=bsend.at[c], recv_sem=brecv.at[c],
            device_id={"ctx": down}, device_id_type=MESH,
        )

    def states(c):
        for j in range(per):
            h = c * per + j
            cols = columns(h)
            step = steps(h)
            between = jnp.where(row > col, step, 0.0).astype(bf16)
            step = step.astype(bf16)
            sums = mm(lower, pair([step, between], 1), 1, 0)
            ec = jnp.exp(sums[:, :width])
            er = jnp.exp(mm(upper, step, 1, 0))
            ecum[h] = ec
            erest[h] = er
            etot[h] = jnp.broadcast_to(ec[tokens - 1 :, :], etot.shape[1:])
            weights[h] = jnp.where(causal, jnp.exp(sums[:, width:]), 0.0)
            v, g = v_ref[:, cols], g_ref[:, cols]
            k_scaled = k_ref[:, cols].astype(jnp.float32) * er
            fout[h] = mm(pair(split(k_scaled), 0), pair([v, v], 0), 0, 0)
            q_scaled = q_ref[:, cols].astype(jnp.float32) * ec
            bout[h] = mm(pair(split(q_scaled), 0), pair([g, g], 0), 0, 0)

    def forward(c):
        @pl.when(me == 0)
        def _():
            for j in range(per):
                fin[c * per + j] = jnp.zeros((width, width), jnp.float32)

        @pl.when(me > 0)
        def _():
            forward_copy(c).wait_recv()

        @pl.when(me < n - 1)
        def _():
            for j in range(per):
                h = c * per + j
                fout[h] = fout[h] + etot[h][:1, :] * fin[h]
            forward_copy(c).start()

    def backward(c):
        @pl.when(me == n - 1)
        def _():
            for j in range(per):
                bin_[c * per + j] = jnp.zeros((width, width), jnp.float32)

        @pl.when(me < n - 1)
        def _():
            backward_copy(c).wait_recv()

        @pl.when(me > 0)
        def _():
            for j in range(per):
                h = c * per + j
                bout[h] = bout[h] + etot[h][:1, :] * bin_[h]
            backward_copy(c).start()

    def intra(c):
        for j in range(per):
            h = c * per + j
            cols = columns(h)
            q, k, v, g = q_ref[:, cols], k_ref[:, cols], v_ref[:, cols], g_ref[:, cols]
            weight = weights[h]
            scores = split(mm(q, k, 1, 1) * weight)
            grad_scores = split(mm(g, v, 1, 1) * weight)
            att0[:, cols] = mm(pair(scores, 1), pair([v, v], 0), 1, 0)
            dq0[:, cols] = mm(pair(grad_scores, 1), pair([k, k], 0), 1, 0)
            dk0[:, cols] = mm(pair(grad_scores, 0), pair([q, q], 0), 0, 0)
            dv0[:, cols] = mm(pair(scores, 0), pair([g, g], 0), 0, 0)

    def cross(c):
        for j in range(per):
            h = c * per + j
            cols = columns(h)
            q, k, v, g = q_ref[:, cols], k_ref[:, cols], v_ref[:, cols], g_ref[:, cols]
            ec, er = ecum[h], erest[h]
            before, after = split(fin[h]), split(bin_[h])
            att = mm(pair([q, q], 1), pair(before, 0), 1, 0)
            att_ref[:, cols] = (att0[:, cols] + ec * att).astype(bf16)
            dq = mm(pair([g, g], 1), pair(before, 1), 1, 1)
            dq_ref[:, cols] = (dq0[:, cols] + ec * dq).astype(bf16)
            dk = mm(pair([v, v], 1), pair(after, 1), 1, 1)
            dk_ref[:, cols] = (dk0[:, cols] + er * dk).astype(bf16)
            dv = mm(pair([k, k], 1), pair(after, 0), 1, 0)
            dv_ref[:, cols] = (dv0[:, cols] + er * dv).astype(bf16)

    def guarded(c, work):
        @pl.when((c >= 0) & (c < chunks))
        def _():
            work(c)

    def tick(t, carry):
        guarded(t, states)
        guarded(t - LAG * me, forward)
        guarded(t - LAG * (n - 1 - me), backward)
        guarded(t, intra)
        guarded(t - LAG * jnp.maximum(me, n - 1 - me), cross)
        return carry

    lax.fori_loop(0, chunks + LAG * (n - 1), tick, 0)

    def drain(c, carry):
        @pl.when(me < n - 1)
        def _():
            forward_copy(c).wait_send()

        @pl.when(me > 0)
        def _():
            backward_copy(c).wait_send()

        return carry

    lax.fori_loop(0, chunks, drain, 0)


def solution(mesh):
    n = mesh.shape["ctx"]

    def shards(queries, key_vectors, values, out_grad, log_decay):
        tokens, heads = log_decay.shape
        total = queries.shape[1]
        width = total // heads
        per = HEADS_PER_CHUNK
        chunks = heads // per
        f32 = jnp.float32
        vmem = pl.BlockSpec(memory_space=pltpu.VMEM)
        state = pltpu.VMEM((heads, width, width), f32)
        decay = pltpu.VMEM((heads, tokens, width), f32)
        rows = pltpu.VMEM((tokens, total), f32)
        sems = pltpu.SemaphoreType.DMA((chunks,))
        return pl.pallas_call(
            functools.partial(kernel, n, per),
            out_shape=[jax.ShapeDtypeStruct((tokens, total), jnp.bfloat16)] * 4,
            in_specs=[vmem] * 5,
            out_specs=[vmem] * 4,
            scratch_shapes=[state] * 4
            + [decay] * 3
            + [pltpu.VMEM((heads, 8, width), f32)]
            + [rows] * 4
            + [sems] * 4,
            compiler_params=pltpu.CompilerParams(
                collective_id=0, has_side_effects=True, vmem_limit_bytes=48 * 1024 * 1024
            ),
        )(queries, key_vectors, values, out_grad, log_decay)

    spec = P(("dp", "ctx"), None)
    return jax.shard_map(
        shards, mesh=mesh, in_specs=(spec,) * 5, out_specs=(spec,) * 4, check_vma=False
    )
```

```python
import functools

import jax
import jax.numpy as jnp
from jax import lax
from jax.experimental import pallas as pl
from jax.experimental.pallas import tpu as pltpu
from jax.sharding import PartitionSpec as P

MESH = pl.DeviceIdType.MESH
HEADS_PER_CHUNK = 2
LAG = 2
GROUPS = 4


def mm(a, b, ca, cb):
    return lax.dot_general(
        a, b, (((ca,), (cb,)), ((), ())), preferred_element_type=jnp.float32
    )


def split(x):
    high = x.astype(jnp.bfloat16)
    return high, (x - high.astype(jnp.float32)).astype(jnp.bfloat16)


def pair(parts, axis):
    return jnp.concatenate(parts, axis=axis)


def kernel(
    n, per, q_hbm, k_hbm, v_hbm, g_hbm, ld_ref, att_ref, dq_ref, dk_ref, dv_ref,
    q_ref, k_ref, v_ref, g_ref, fin, fout, bin_, bout, ecum, erest, weights, etot, att0, dq0, dk0, dv0,
    fsend, frecv, bsend, brecv, loaded,
):
    me = lax.axis_index("ctx")
    up, down = lax.rem(me + 1, n), lax.rem(me + n - 1, n)
    tokens, heads = ld_ref.shape
    width = q_hbm.shape[1] // heads
    chunks = heads // per
    bf16 = jnp.bfloat16

    span = heads * width // GROUPS
    chunks_per_group = chunks // GROUPS

    def loads(group):
        cols = pl.ds(pl.multiple_of(group * span, span), span)
        arrays = ((q_hbm, q_ref), (k_hbm, k_ref), (v_hbm, v_ref), (g_hbm, g_ref))
        return [
            pltpu.make_async_copy(src.at[:, cols], dst.at[:, cols], loaded.at[i, group])
            for i, (src, dst) in enumerate(arrays)
        ]

    for group in range(GROUPS):
        for load in loads(group):
            load.start()

    barrier = pltpu.get_barrier_semaphore()

    @pl.when(me > 0)
    def _():
        pl.semaphore_signal(barrier, inc=1, device_id={"ctx": down}, device_id_type=MESH)

    @pl.when(me < n - 1)
    def _():
        pl.semaphore_signal(barrier, inc=1, device_id={"ctx": up}, device_id_type=MESH)

    pl.semaphore_wait(barrier, jnp.minimum(me, 1) + jnp.minimum(n - 1 - me, 1))

    row = lax.broadcasted_iota(jnp.int32, (tokens, tokens), 0)
    col = lax.broadcasted_iota(jnp.int32, (tokens, tokens), 1)
    causal = row >= col
    lower = jnp.where(causal, 1.0, 0.0).astype(bf16)
    upper = jnp.where(row < col, 1.0, 0.0).astype(bf16)
    head_row = lax.broadcasted_iota(jnp.int32, (heads, width), 0)

    def columns(h):
        return pl.ds(pl.multiple_of(h * width, width), width)

    def steps(h):
        pick = jnp.where(head_row == h, 1.0, 0.0).astype(bf16)
        return mm(ld_ref[...], pick, 1, 0)

    def forward_copy(c):
        part = pl.ds(c * per, per)
        return pltpu.make_async_remote_copy(
            src_ref=fout.at[part], dst_ref=fin.at[part],
            send_sem=fsend.at[c], recv_sem=frecv.at[c],
            device_id={"ctx": up}, device_id_type=MESH,
        )

    def backward_copy(c):
        part = pl.ds(c * per, per)
        return pltpu.make_async_remote_copy(
            src_ref=bout.at[part], dst_ref=bin_.at[part],
            send_sem=bsend.at[c], recv_sem=brecv.at[c],
            device_id={"ctx": down}, device_id_type=MESH,
        )

    def arrive(c):
        @pl.when(lax.rem(c, chunks_per_group) == 0)
        def _():
            for load in loads(lax.div(c, chunks_per_group)):
                load.wait()

    def states(c):
        for j in range(per):
            h = c * per + j
            cols = columns(h)
            step = steps(h)
            between = jnp.where(row > col, step, 0.0).astype(bf16)
            step = step.astype(bf16)
            sums = mm(lower, pair([step, between], 1), 1, 0)
            ec = jnp.exp(sums[:, :width])
            er = jnp.exp(mm(upper, step, 1, 0))
            ecum[h] = ec
            erest[h] = er
            etot[h] = jnp.broadcast_to(ec[tokens - 1 :, :], etot.shape[1:])
            weights[h] = jnp.where(causal, jnp.exp(sums[:, width:]), 0.0)
            v, g = v_ref[:, cols], g_ref[:, cols]
            k_scaled = k_ref[:, cols].astype(jnp.float32) * er
            fout[h] = mm(pair(split(k_scaled), 0), pair([v, v], 0), 0, 0)
            q_scaled = q_ref[:, cols].astype(jnp.float32) * ec
            bout[h] = mm(pair(split(q_scaled), 0), pair([g, g], 0), 0, 0)

    def forward(c):
        @pl.when(me == 0)
        def _():
            for j in range(per):
                fin[c * per + j] = jnp.zeros((width, width), jnp.float32)

        @pl.when(me > 0)
        def _():
            forward_copy(c).wait_recv()

        @pl.when(me < n - 1)
        def _():
            for j in range(per):
                h = c * per + j
                fout[h] = fout[h] + etot[h][:1, :] * fin[h]
            forward_copy(c).start()

    def backward(c):
        @pl.when(me == n - 1)
        def _():
            for j in range(per):
                bin_[c * per + j] = jnp.zeros((width, width), jnp.float32)

        @pl.when(me < n - 1)
        def _():
            backward_copy(c).wait_recv()

        @pl.when(me > 0)
        def _():
            for j in range(per):
                h = c * per + j
                bout[h] = bout[h] + etot[h][:1, :] * bin_[h]
            backward_copy(c).start()

    def intra(c):
        for j in range(per):
            h = c * per + j
            cols = columns(h)
            q, k, v, g = q_ref[:, cols], k_ref[:, cols], v_ref[:, cols], g_ref[:, cols]
            weight = weights[h]
            scores = split(mm(q, k, 1, 1) * weight)
            grad_scores = split(mm(g, v, 1, 1) * weight)
            att0[:, cols] = mm(pair(scores, 1), pair([v, v], 0), 1, 0)
            dq0[:, cols] = mm(pair(grad_scores, 1), pair([k, k], 0), 1, 0)
            dk0[:, cols] = mm(pair(grad_scores, 0), pair([q, q], 0), 0, 0)
            dv0[:, cols] = mm(pair(scores, 0), pair([g, g], 0), 0, 0)

    def cross(c):
        for j in range(per):
            h = c * per + j
            cols = columns(h)
            q, k, v, g = q_ref[:, cols], k_ref[:, cols], v_ref[:, cols], g_ref[:, cols]
            ec, er = ecum[h], erest[h]
            before, after = split(fin[h]), split(bin_[h])
            att = mm(pair([q, q], 1), pair(before, 0), 1, 0)
            att_ref[:, cols] = (att0[:, cols] + ec * att).astype(bf16)
            dq = mm(pair([g, g], 1), pair(before, 1), 1, 1)
            dq_ref[:, cols] = (dq0[:, cols] + ec * dq).astype(bf16)
            dk = mm(pair([v, v], 1), pair(after, 1), 1, 1)
            dk_ref[:, cols] = (dk0[:, cols] + er * dk).astype(bf16)
            dv = mm(pair([k, k], 1), pair(after, 0), 1, 0)
            dv_ref[:, cols] = (dv0[:, cols] + er * dv).astype(bf16)

    def guarded(c, work):
        @pl.when((c >= 0) & (c < chunks))
        def _():
            work(c)

    def tick(t, carry):
        guarded(t, arrive)
        guarded(t, states)
        guarded(t - LAG * me, forward)
        guarded(t - LAG * (n - 1 - me), backward)
        guarded(t, intra)
        guarded(t - LAG * jnp.maximum(me, n - 1 - me), cross)
        return carry

    lax.fori_loop(0, chunks + LAG * (n - 1), tick, 0)

    def drain(c, carry):
        @pl.when(me < n - 1)
        def _():
            forward_copy(c).wait_send()

        @pl.when(me > 0)
        def _():
            backward_copy(c).wait_send()

        return carry

    lax.fori_loop(0, chunks, drain, 0)


def solution(mesh):
    n = mesh.shape["ctx"]

    def shards(queries, key_vectors, values, out_grad, log_decay):
        tokens, heads = log_decay.shape
        total = queries.shape[1]
        width = total // heads
        per = HEADS_PER_CHUNK
        chunks = heads // per
        f32 = jnp.float32
        vmem = pl.BlockSpec(memory_space=pltpu.VMEM)
        state = pltpu.VMEM((heads, width, width), f32)
        decay = pltpu.VMEM((heads, tokens, width), f32)
        rows = pltpu.VMEM((tokens, total), f32)
        sems = pltpu.SemaphoreType.DMA((chunks,))
        return pl.pallas_call(
            functools.partial(kernel, n, per),
            out_shape=[jax.ShapeDtypeStruct((tokens, total), jnp.bfloat16)] * 4,
            in_specs=[pl.BlockSpec(memory_space=pltpu.HBM)] * 4 + [vmem],
            out_specs=[vmem] * 4,
            scratch_shapes=[pltpu.VMEM((tokens, total), jnp.bfloat16)] * 4
            + [state] * 4
            + [decay] * 3
            + [pltpu.VMEM((heads, 8, width), f32)]
            + [rows] * 4
            + [sems] * 4
            + [pltpu.SemaphoreType.DMA((4, GROUPS))],
            compiler_params=pltpu.CompilerParams(
                collective_id=0, has_side_effects=True, vmem_limit_bytes=48 * 1024 * 1024
            ),
        )(queries, key_vectors, values, out_grad, log_decay)

    spec = P(("dp", "ctx"), None)
    return jax.shard_map(
        shards, mesh=mesh, in_specs=(spec,) * 5, out_specs=(spec,) * 4, check_vma=False
    )
```

```python
import functools

import jax
import jax.numpy as jnp
from jax import lax
from jax.experimental import pallas as pl
from jax.experimental.pallas import tpu as pltpu
from jax.sharding import PartitionSpec as P

MESH = pl.DeviceIdType.MESH
HEADS_PER_CHUNK = 2
LAG = 2
GROUPS = 4


def mm(a, b, ca, cb):
    return lax.dot_general(
        a, b, (((ca,), (cb,)), ((), ())), preferred_element_type=jnp.float32
    )


def split(x):
    high = x.astype(jnp.bfloat16)
    return high, (x - high.astype(jnp.float32)).astype(jnp.bfloat16)


def pair(parts, axis):
    return jnp.concatenate(parts, axis=axis)


def kernel(
    n, per, q_hbm, k_hbm, v_hbm, g_hbm, ld_ref, att_ref, dq_ref, dk_ref, dv_ref,
    q_ref, k_ref, v_ref, g_ref, fin, fout, bin_, bout, ecum, erest, weights, etot, att0, dq0, dk0, dv0,
    fsend, frecv, bsend, brecv, loaded,
):
    me = lax.axis_index("ctx")
    up, down = lax.rem(me + 1, n), lax.rem(me + n - 1, n)
    tokens, heads = ld_ref.shape
    width = q_hbm.shape[1] // heads
    chunks = heads // per
    bf16 = jnp.bfloat16

    span = heads * width // GROUPS
    chunks_per_group = chunks // GROUPS

    def loads(group):
        cols = pl.ds(pl.multiple_of(group * span, span), span)
        arrays = ((q_hbm, q_ref), (k_hbm, k_ref), (v_hbm, v_ref), (g_hbm, g_ref))
        return [
            pltpu.make_async_copy(src.at[:, cols], dst.at[:, cols], loaded.at[i, group])
            for i, (src, dst) in enumerate(arrays)
        ]

    for group in range(GROUPS):
        for load in loads(group):
            load.start()

    barrier = pltpu.get_barrier_semaphore()

    @pl.when(me > 0)
    def _():
        pl.semaphore_signal(barrier, inc=1, device_id={"ctx": down}, device_id_type=MESH)

    @pl.when(me < n - 1)
    def _():
        pl.semaphore_signal(barrier, inc=1, device_id={"ctx": up}, device_id_type=MESH)

    pl.semaphore_wait(barrier, jnp.minimum(me, 1) + jnp.minimum(n - 1 - me, 1))

    row = lax.broadcasted_iota(jnp.int32, (tokens, tokens), 0)
    col = lax.broadcasted_iota(jnp.int32, (tokens, tokens), 1)
    causal = row >= col
    lower = jnp.where(causal, 1.0, 0.0).astype(bf16)
    upper = jnp.where(row < col, 1.0, 0.0).astype(bf16)
    head_row = lax.broadcasted_iota(jnp.int32, (heads, width), 0)

    def columns(h):
        return pl.ds(pl.multiple_of(h * width, width), width)

    def steps(h):
        pick = jnp.where(head_row == h, 1.0, 0.0).astype(bf16)
        return mm(ld_ref[...], pick, 1, 0)

    def forward_copy(c):
        part = pl.ds(c * per, per)
        return pltpu.make_async_remote_copy(
            src_ref=fout.at[part], dst_ref=fin.at[part],
            send_sem=fsend.at[c], recv_sem=frecv.at[c],
            device_id={"ctx": up}, device_id_type=MESH,
        )

    def backward_copy(c):
        part = pl.ds(c * per, per)
        return pltpu.make_async_remote_copy(
            src_ref=bout.at[part], dst_ref=bin_.at[part],
            send_sem=bsend.at[c], recv_sem=brecv.at[c],
            device_id={"ctx": down}, device_id_type=MESH,
        )

    def arrive(c):
        @pl.when(lax.rem(c, chunks_per_group) == 0)
        def _():
            for load in loads(lax.div(c, chunks_per_group)):
                load.wait()

    def states(c):
        for j in range(per):
            h = c * per + j
            cols = columns(h)
            step = steps(h)
            between = jnp.where(row > col, step, 0.0).astype(bf16)
            step = step.astype(bf16)
            sums = mm(lower, pair([step, between], 1), 1, 0)
            ec = jnp.exp(sums[:, :width])
            er = jnp.exp(mm(upper, step, 1, 0))
            ecum[h] = ec
            erest[h] = er
            etot[h] = jnp.broadcast_to(ec[tokens - 1 :, :], etot.shape[1:])
            weights[h] = jnp.where(causal, jnp.exp(sums[:, width:]), 0.0)
            v, g = v_ref[:, cols], g_ref[:, cols]
            k_scaled = k_ref[:, cols].astype(jnp.float32) * er
            fout[h] = mm(pair(split(k_scaled), 0), pair([v, v], 0), 0, 0)
            q_scaled = q_ref[:, cols].astype(jnp.float32) * ec
            bout[h] = mm(pair(split(q_scaled), 0), pair([g, g], 0), 0, 0)

    def forward(c):
        @pl.when(me == 0)
        def _():
            for j in range(per):
                fin[c * per + j] = jnp.zeros((width, width), jnp.float32)

        @pl.when(me > 0)
        def _():
            forward_copy(c).wait_recv()

        @pl.when(me < n - 1)
        def _():
            for j in range(per):
                h = c * per + j
                fout[h] = fout[h] + etot[h][:1, :] * fin[h]
            forward_copy(c).start()

    def backward(c):
        @pl.when(me == n - 1)
        def _():
            for j in range(per):
                bin_[c * per + j] = jnp.zeros((width, width), jnp.float32)

        @pl.when(me < n - 1)
        def _():
            backward_copy(c).wait_recv()

        @pl.when(me > 0)
        def _():
            for j in range(per):
                h = c * per + j
                bout[h] = bout[h] + etot[h][:1, :] * bin_[h]
            backward_copy(c).start()

    def intra(c):
        for j in range(per):
            h = c * per + j
            cols = columns(h)
            q, k, v, g = q_ref[:, cols], k_ref[:, cols], v_ref[:, cols], g_ref[:, cols]
            weight = weights[h]
            scores = split(mm(q, k, 1, 1) * weight)
            grad_scores = split(mm(g, v, 1, 1) * weight)
            att0[:, cols] = mm(pair(scores, 1), pair([v, v], 0), 1, 0)
            dq0[:, cols] = mm(pair(grad_scores, 1), pair([k, k], 0), 1, 0)
            dk0[:, cols] = mm(pair(grad_scores, 0), pair([q, q], 0), 0, 0)
            dv0[:, cols] = mm(pair(scores, 0), pair([g, g], 0), 0, 0)

    def cross(c):
        for j in range(per):
            h = c * per + j
            cols = columns(h)
            q, k, v, g = q_ref[:, cols], k_ref[:, cols], v_ref[:, cols], g_ref[:, cols]
            ec, er = ecum[h], erest[h]
            before, after = split(fin[h]), split(bin_[h])
            att = mm(pair([q, q], 1), pair(before, 0), 1, 0)
            att_ref[:, cols] = (att0[:, cols] + ec * att).astype(bf16)
            dq = mm(pair([g, g], 1), pair(before, 1), 1, 1)
            dq_ref[:, cols] = (dq0[:, cols] + ec * dq).astype(bf16)
            dk = mm(pair([v, v], 1), pair(after, 1), 1, 1)
            dk_ref[:, cols] = (dk0[:, cols] + er * dk).astype(bf16)
            dv = mm(pair([k, k], 1), pair(after, 0), 1, 0)
            dv_ref[:, cols] = (dv0[:, cols] + er * dv).astype(bf16)

    def guarded(c, work):
        @pl.when((c >= 0) & (c < chunks))
        def _():
            work(c)

    def local(c):
        states(c)
        intra(c)

    def tick(t, carry):
        guarded(t - 1 - LAG * me, forward)
        guarded(t - 1 - LAG * (n - 1 - me), backward)
        guarded(t, arrive)
        late = t - 1 - LAG * jnp.maximum(me, n - 1 - me)
        crossing = (late >= 0) & (late < chunks)

        @pl.when((t < chunks) & crossing)
        def _():
            local(t)
            cross(late)

        @pl.when((t < chunks) & ((late < 0) | (late >= chunks)))
        def _():
            local(t)

        @pl.when((t >= chunks) & crossing)
        def _():
            cross(late)

        return carry

    lax.fori_loop(0, chunks + LAG * (n - 1) + 1, tick, 0)

    def drain(c, carry):
        @pl.when(me < n - 1)
        def _():
            forward_copy(c).wait_send()

        @pl.when(me > 0)
        def _():
            backward_copy(c).wait_send()

        return carry

    lax.fori_loop(0, chunks, drain, 0)


def solution(mesh):
    n = mesh.shape["ctx"]

    def shards(queries, key_vectors, values, out_grad, log_decay):
        tokens, heads = log_decay.shape
        total = queries.shape[1]
        width = total // heads
        per = HEADS_PER_CHUNK
        chunks = heads // per
        f32 = jnp.float32
        vmem = pl.BlockSpec(memory_space=pltpu.VMEM)
        state = pltpu.VMEM((heads, width, width), f32)
        decay = pltpu.VMEM((heads, tokens, width), f32)
        rows = pltpu.VMEM((tokens, total), f32)
        sems = pltpu.SemaphoreType.DMA((chunks,))
        return pl.pallas_call(
            functools.partial(kernel, n, per),
            out_shape=[jax.ShapeDtypeStruct((tokens, total), jnp.bfloat16)] * 4,
            in_specs=[pl.BlockSpec(memory_space=pltpu.HBM)] * 4 + [vmem],
            out_specs=[vmem] * 4,
            scratch_shapes=[pltpu.VMEM((tokens, total), jnp.bfloat16)] * 4
            + [state] * 4
            + [decay] * 3
            + [pltpu.VMEM((heads, 8, width), f32)]
            + [rows] * 4
            + [sems] * 4
            + [pltpu.SemaphoreType.DMA((4, GROUPS))],
            compiler_params=pltpu.CompilerParams(
                collective_id=0, has_side_effects=True, vmem_limit_bytes=48 * 1024 * 1024
            ),
        )(queries, key_vectors, values, out_grad, log_decay)

    spec = P(("dp", "ctx"), None)
    return jax.shard_map(
        shards, mesh=mesh, in_specs=(spec,) * 5, out_specs=(spec,) * 4, check_vma=False
    )
```

```python
import functools

import jax
import jax.numpy as jnp
from jax import lax
from jax.experimental import pallas as pl
from jax.experimental.pallas import tpu as pltpu
from jax.sharding import PartitionSpec as P

MESH = pl.DeviceIdType.MESH
HEADS_PER_CHUNK = 1
LAG = 2
GROUPS = 4


def mm(a, b, ca, cb):
    return lax.dot_general(
        a, b, (((ca,), (cb,)), ((), ())), preferred_element_type=jnp.float32
    )


def split(x):
    high = x.astype(jnp.bfloat16)
    return high, (x - high.astype(jnp.float32)).astype(jnp.bfloat16)


def pair(parts, axis):
    return jnp.concatenate(parts, axis=axis)


def kernel(
    n, per, q_hbm, k_hbm, v_hbm, g_hbm, ld_ref, att_ref, dq_ref, dk_ref, dv_ref,
    q_ref, k_ref, v_ref, g_ref, fin, fout, bin_, bout, ecum, erest, weights, etot, att0, dq0, dk0, dv0,
    fsend, frecv, bsend, brecv, loaded,
):
    me = lax.axis_index("ctx")
    up, down = lax.rem(me + 1, n), lax.rem(me + n - 1, n)
    tokens, heads = ld_ref.shape
    width = q_hbm.shape[1] // heads
    chunks = heads // per
    bf16 = jnp.bfloat16

    span = heads * width // GROUPS
    chunks_per_group = chunks // GROUPS

    def loads(group):
        cols = pl.ds(pl.multiple_of(group * span, span), span)
        arrays = ((q_hbm, q_ref), (k_hbm, k_ref), (v_hbm, v_ref), (g_hbm, g_ref))
        return [
            pltpu.make_async_copy(src.at[:, cols], dst.at[:, cols], loaded.at[i, group])
            for i, (src, dst) in enumerate(arrays)
        ]

    for group in range(GROUPS):
        for load in loads(group):
            load.start()

    barrier = pltpu.get_barrier_semaphore()

    @pl.when(me > 0)
    def _():
        pl.semaphore_signal(barrier, inc=1, device_id={"ctx": down}, device_id_type=MESH)

    @pl.when(me < n - 1)
    def _():
        pl.semaphore_signal(barrier, inc=1, device_id={"ctx": up}, device_id_type=MESH)

    pl.semaphore_wait(barrier, jnp.minimum(me, 1) + jnp.minimum(n - 1 - me, 1))

    row = lax.broadcasted_iota(jnp.int32, (tokens, tokens), 0)
    col = lax.broadcasted_iota(jnp.int32, (tokens, tokens), 1)
    causal = row >= col
    lower = jnp.where(causal, 1.0, 0.0).astype(bf16)
    upper = jnp.where(row < col, 1.0, 0.0).astype(bf16)
    head_row = lax.broadcasted_iota(jnp.int32, (heads, width), 0)

    def columns(h):
        return pl.ds(pl.multiple_of(h * width, width), width)

    def steps(h):
        pick = jnp.where(head_row == h, 1.0, 0.0).astype(bf16)
        return mm(ld_ref[...], pick, 1, 0)

    def forward_copy(c):
        part = pl.ds(c * per, per)
        return pltpu.make_async_remote_copy(
            src_ref=fout.at[part], dst_ref=fin.at[part],
            send_sem=fsend.at[c], recv_sem=frecv.at[c],
            device_id={"ctx": up}, device_id_type=MESH,
        )

    def backward_copy(c):
        part = pl.ds(c * per, per)
        return pltpu.make_async_remote_copy(
            src_ref=bout.at[part], dst_ref=bin_.at[part],
            send_sem=bsend.at[c], recv_sem=brecv.at[c],
            device_id={"ctx": down}, device_id_type=MESH,
        )

    def arrive(c):
        @pl.when(lax.rem(c, chunks_per_group) == 0)
        def _():
            for load in loads(lax.div(c, chunks_per_group)):
                load.wait()

    def states(c):
        for j in range(per):
            h = c * per + j
            cols = columns(h)
            step = steps(h)
            between = jnp.where(row > col, step, 0.0).astype(bf16)
            step = step.astype(bf16)
            sums = mm(lower, pair([step, between], 1), 1, 0)
            ec = jnp.exp(sums[:, :width])
            er = jnp.exp(mm(upper, step, 1, 0))
            ecum[h] = ec
            erest[h] = er
            etot[h] = jnp.broadcast_to(ec[tokens - 1 :, :], etot.shape[1:])
            weights[h] = jnp.where(causal, jnp.exp(sums[:, width:]), 0.0)
            v, g = v_ref[:, cols], g_ref[:, cols]
            k_scaled = k_ref[:, cols].astype(jnp.float32) * er
            fout[h] = mm(pair(split(k_scaled), 0), pair([v, v], 0), 0, 0)
            q_scaled = q_ref[:, cols].astype(jnp.float32) * ec
            bout[h] = mm(pair(split(q_scaled), 0), pair([g, g], 0), 0, 0)

    def forward(c):
        @pl.when(me == 0)
        def _():
            for j in range(per):
                fin[c * per + j] = jnp.zeros((width, width), jnp.float32)

        @pl.when(me > 0)
        def _():
            forward_copy(c).wait_recv()

        @pl.when(me < n - 1)
        def _():
            for j in range(per):
                h = c * per + j
                fout[h] = fout[h] + etot[h][:1, :] * fin[h]
            forward_copy(c).start()

    def backward(c):
        @pl.when(me == n - 1)
        def _():
            for j in range(per):
                bin_[c * per + j] = jnp.zeros((width, width), jnp.float32)

        @pl.when(me < n - 1)
        def _():
            backward_copy(c).wait_recv()

        @pl.when(me > 0)
        def _():
            for j in range(per):
                h = c * per + j
                bout[h] = bout[h] + etot[h][:1, :] * bin_[h]
            backward_copy(c).start()

    def intra(c):
        for j in range(per):
            h = c * per + j
            cols = columns(h)
            q, k, v, g = q_ref[:, cols], k_ref[:, cols], v_ref[:, cols], g_ref[:, cols]
            weight = weights[h]
            scores = split(mm(q, k, 1, 1) * weight)
            grad_scores = split(mm(g, v, 1, 1) * weight)
            att0[:, cols] = mm(pair(scores, 1), pair([v, v], 0), 1, 0)
            dq0[:, cols] = mm(pair(grad_scores, 1), pair([k, k], 0), 1, 0)
            dk0[:, cols] = mm(pair(grad_scores, 0), pair([q, q], 0), 0, 0)
            dv0[:, cols] = mm(pair(scores, 0), pair([g, g], 0), 0, 0)

    def cross(c):
        for j in range(per):
            h = c * per + j
            cols = columns(h)
            q, k, v, g = q_ref[:, cols], k_ref[:, cols], v_ref[:, cols], g_ref[:, cols]
            ec, er = ecum[h], erest[h]
            before, after = split(fin[h]), split(bin_[h])
            att = mm(pair([q, q], 1), pair(before, 0), 1, 0)
            att_ref[:, cols] = (att0[:, cols] + ec * att).astype(bf16)
            dq = mm(pair([g, g], 1), pair(before, 1), 1, 1)
            dq_ref[:, cols] = (dq0[:, cols] + ec * dq).astype(bf16)
            dk = mm(pair([v, v], 1), pair(after, 1), 1, 1)
            dk_ref[:, cols] = (dk0[:, cols] + er * dk).astype(bf16)
            dv = mm(pair([k, k], 1), pair(after, 0), 1, 0)
            dv_ref[:, cols] = (dv0[:, cols] + er * dv).astype(bf16)

    def guarded(c, work):
        @pl.when((c >= 0) & (c < chunks))
        def _():
            work(c)

    def local(c):
        states(c)
        intra(c)

    def tick(t, carry):
        guarded(t - 1 - LAG * me, forward)
        guarded(t - 1 - LAG * (n - 1 - me), backward)
        guarded(t, arrive)
        late = t - 1 - LAG * jnp.maximum(me, n - 1 - me)
        crossing = (late >= 0) & (late < chunks)

        @pl.when((t < chunks) & crossing)
        def _():
            local(t)
            cross(late)

        @pl.when((t < chunks) & ((late < 0) | (late >= chunks)))
        def _():
            local(t)

        @pl.when((t >= chunks) & crossing)
        def _():
            cross(late)

        return carry

    lax.fori_loop(0, chunks + LAG * (n - 1) + 1, tick, 0)

    def drain(c, carry):
        @pl.when(me < n - 1)
        def _():
            forward_copy(c).wait_send()

        @pl.when(me > 0)
        def _():
            backward_copy(c).wait_send()

        return carry

    lax.fori_loop(0, chunks, drain, 0)


def solution(mesh):
    n = mesh.shape["ctx"]

    def shards(queries, key_vectors, values, out_grad, log_decay):
        tokens, heads = log_decay.shape
        total = queries.shape[1]
        width = total // heads
        per = HEADS_PER_CHUNK
        chunks = heads // per
        f32 = jnp.float32
        vmem = pl.BlockSpec(memory_space=pltpu.VMEM)
        state = pltpu.VMEM((heads, width, width), f32)
        decay = pltpu.VMEM((heads, tokens, width), f32)
        rows = pltpu.VMEM((tokens, total), f32)
        sems = pltpu.SemaphoreType.DMA((chunks,))
        return pl.pallas_call(
            functools.partial(kernel, n, per),
            out_shape=[jax.ShapeDtypeStruct((tokens, total), jnp.bfloat16)] * 4,
            in_specs=[pl.BlockSpec(memory_space=pltpu.HBM)] * 4 + [vmem],
            out_specs=[vmem] * 4,
            scratch_shapes=[pltpu.VMEM((tokens, total), jnp.bfloat16)] * 4
            + [state] * 4
            + [decay] * 3
            + [pltpu.VMEM((heads, 8, width), f32)]
            + [rows] * 4
            + [sems] * 4
            + [pltpu.SemaphoreType.DMA((4, GROUPS))],
            compiler_params=pltpu.CompilerParams(
                collective_id=0, has_side_effects=True, vmem_limit_bytes=48 * 1024 * 1024
            ),
        )(queries, key_vectors, values, out_grad, log_decay)

    spec = P(("dp", "ctx"), None)
    return jax.shard_map(
        shards, mesh=mesh, in_specs=(spec,) * 5, out_specs=(spec,) * 4, check_vma=False
    )
```

```python
import functools

import jax
import jax.numpy as jnp
from jax import lax
from jax.experimental import pallas as pl
from jax.experimental.pallas import tpu as pltpu
from jax.sharding import PartitionSpec as P

MESH = pl.DeviceIdType.MESH
HEADS_PER_CHUNK = 4
LAG = 2
GROUPS = 4


def mm(a, b, ca, cb):
    return lax.dot_general(
        a, b, (((ca,), (cb,)), ((), ())), preferred_element_type=jnp.float32
    )


def split(x):
    high = x.astype(jnp.bfloat16)
    return high, (x - high.astype(jnp.float32)).astype(jnp.bfloat16)


def pair(parts, axis):
    return jnp.concatenate(parts, axis=axis)


def kernel(
    n, per, q_hbm, k_hbm, v_hbm, g_hbm, ld_ref, att_ref, dq_ref, dk_ref, dv_ref,
    q_ref, k_ref, v_ref, g_ref, fin, fout, bin_, bout, ecum, erest, weights, etot, att0, dq0, dk0, dv0,
    fsend, frecv, bsend, brecv, loaded,
):
    me = lax.axis_index("ctx")
    up, down = lax.rem(me + 1, n), lax.rem(me + n - 1, n)
    tokens, heads = ld_ref.shape
    width = q_hbm.shape[1] // heads
    chunks = heads // per
    bf16 = jnp.bfloat16

    span = heads * width // GROUPS
    chunks_per_group = chunks // GROUPS

    def loads(group):
        cols = pl.ds(pl.multiple_of(group * span, span), span)
        arrays = ((q_hbm, q_ref), (k_hbm, k_ref), (v_hbm, v_ref), (g_hbm, g_ref))
        return [
            pltpu.make_async_copy(src.at[:, cols], dst.at[:, cols], loaded.at[i, group])
            for i, (src, dst) in enumerate(arrays)
        ]

    for group in range(GROUPS):
        for load in loads(group):
            load.start()

    barrier = pltpu.get_barrier_semaphore()

    @pl.when(me > 0)
    def _():
        pl.semaphore_signal(barrier, inc=1, device_id={"ctx": down}, device_id_type=MESH)

    @pl.when(me < n - 1)
    def _():
        pl.semaphore_signal(barrier, inc=1, device_id={"ctx": up}, device_id_type=MESH)

    pl.semaphore_wait(barrier, jnp.minimum(me, 1) + jnp.minimum(n - 1 - me, 1))

    row = lax.broadcasted_iota(jnp.int32, (tokens, tokens), 0)
    col = lax.broadcasted_iota(jnp.int32, (tokens, tokens), 1)
    causal = row >= col
    lower = jnp.where(causal, 1.0, 0.0).astype(bf16)
    upper = jnp.where(row < col, 1.0, 0.0).astype(bf16)
    head_row = lax.broadcasted_iota(jnp.int32, (heads, width), 0)

    def columns(h):
        return pl.ds(pl.multiple_of(h * width, width), width)

    def steps(h):
        pick = jnp.where(head_row == h, 1.0, 0.0).astype(bf16)
        return mm(ld_ref[...], pick, 1, 0)

    def forward_copy(c):
        part = pl.ds(c * per, per)
        return pltpu.make_async_remote_copy(
            src_ref=fout.at[part], dst_ref=fin.at[part],
            send_sem=fsend.at[c], recv_sem=frecv.at[c],
            device_id={"ctx": up}, device_id_type=MESH,
        )

    def backward_copy(c):
        part = pl.ds(c * per, per)
        return pltpu.make_async_remote_copy(
            src_ref=bout.at[part], dst_ref=bin_.at[part],
            send_sem=bsend.at[c], recv_sem=brecv.at[c],
            device_id={"ctx": down}, device_id_type=MESH,
        )

    def arrive(c):
        @pl.when(lax.rem(c, chunks_per_group) == 0)
        def _():
            for load in loads(lax.div(c, chunks_per_group)):
                load.wait()

    def states(c):
        for j in range(per):
            h = c * per + j
            cols = columns(h)
            step = steps(h)
            between = jnp.where(row > col, step, 0.0).astype(bf16)
            step = step.astype(bf16)
            sums = mm(lower, pair([step, between], 1), 1, 0)
            ec = jnp.exp(sums[:, :width])
            er = jnp.exp(mm(upper, step, 1, 0))
            ecum[h] = ec
            erest[h] = er
            etot[h] = jnp.broadcast_to(ec[tokens - 1 :, :], etot.shape[1:])
            weights[h] = jnp.where(causal, jnp.exp(sums[:, width:]), 0.0)
            v, g = v_ref[:, cols], g_ref[:, cols]
            k_scaled = k_ref[:, cols].astype(jnp.float32) * er
            fout[h] = mm(pair(split(k_scaled), 0), pair([v, v], 0), 0, 0)
            q_scaled = q_ref[:, cols].astype(jnp.float32) * ec
            bout[h] = mm(pair(split(q_scaled), 0), pair([g, g], 0), 0, 0)

    def forward(c):
        @pl.when(me == 0)
        def _():
            for j in range(per):
                fin[c * per + j] = jnp.zeros((width, width), jnp.float32)

        @pl.when(me > 0)
        def _():
            forward_copy(c).wait_recv()

        @pl.when(me < n - 1)
        def _():
            for j in range(per):
                h = c * per + j
                fout[h] = fout[h] + etot[h][:1, :] * fin[h]
            forward_copy(c).start()

    def backward(c):
        @pl.when(me == n - 1)
        def _():
            for j in range(per):
                bin_[c * per + j] = jnp.zeros((width, width), jnp.float32)

        @pl.when(me < n - 1)
        def _():
            backward_copy(c).wait_recv()

        @pl.when(me > 0)
        def _():
            for j in range(per):
                h = c * per + j
                bout[h] = bout[h] + etot[h][:1, :] * bin_[h]
            backward_copy(c).start()

    def intra(c):
        for j in range(per):
            h = c * per + j
            cols = columns(h)
            q, k, v, g = q_ref[:, cols], k_ref[:, cols], v_ref[:, cols], g_ref[:, cols]
            weight = weights[h]
            scores = split(mm(q, k, 1, 1) * weight)
            grad_scores = split(mm(g, v, 1, 1) * weight)
            att0[:, cols] = mm(pair(scores, 1), pair([v, v], 0), 1, 0)
            dq0[:, cols] = mm(pair(grad_scores, 1), pair([k, k], 0), 1, 0)
            dk0[:, cols] = mm(pair(grad_scores, 0), pair([q, q], 0), 0, 0)
            dv0[:, cols] = mm(pair(scores, 0), pair([g, g], 0), 0, 0)

    def cross(c):
        for j in range(per):
            h = c * per + j
            cols = columns(h)
            q, k, v, g = q_ref[:, cols], k_ref[:, cols], v_ref[:, cols], g_ref[:, cols]
            ec, er = ecum[h], erest[h]
            before, after = split(fin[h]), split(bin_[h])
            att = mm(pair([q, q], 1), pair(before, 0), 1, 0)
            att_ref[:, cols] = (att0[:, cols] + ec * att).astype(bf16)
            dq = mm(pair([g, g], 1), pair(before, 1), 1, 1)
            dq_ref[:, cols] = (dq0[:, cols] + ec * dq).astype(bf16)
            dk = mm(pair([v, v], 1), pair(after, 1), 1, 1)
            dk_ref[:, cols] = (dk0[:, cols] + er * dk).astype(bf16)
            dv = mm(pair([k, k], 1), pair(after, 0), 1, 0)
            dv_ref[:, cols] = (dv0[:, cols] + er * dv).astype(bf16)

    def guarded(c, work):
        @pl.when((c >= 0) & (c < chunks))
        def _():
            work(c)

    def local(c):
        states(c)
        intra(c)

    def tick(t, carry):
        guarded(t - 1 - LAG * me, forward)
        guarded(t - 1 - LAG * (n - 1 - me), backward)
        guarded(t, arrive)
        late = t - 1 - LAG * jnp.maximum(me, n - 1 - me)
        crossing = (late >= 0) & (late < chunks)

        @pl.when((t < chunks) & crossing)
        def _():
            local(t)
            cross(late)

        @pl.when((t < chunks) & ((late < 0) | (late >= chunks)))
        def _():
            local(t)

        @pl.when((t >= chunks) & crossing)
        def _():
            cross(late)

        return carry

    lax.fori_loop(0, chunks + LAG * (n - 1) + 1, tick, 0)

    def drain(c, carry):
        @pl.when(me < n - 1)
        def _():
            forward_copy(c).wait_send()

        @pl.when(me > 0)
        def _():
            backward_copy(c).wait_send()

        return carry

    lax.fori_loop(0, chunks, drain, 0)


def solution(mesh):
    n = mesh.shape["ctx"]

    def shards(queries, key_vectors, values, out_grad, log_decay):
        tokens, heads = log_decay.shape
        total = queries.shape[1]
        width = total // heads
        per = HEADS_PER_CHUNK
        chunks = heads // per
        f32 = jnp.float32
        vmem = pl.BlockSpec(memory_space=pltpu.VMEM)
        state = pltpu.VMEM((heads, width, width), f32)
        decay = pltpu.VMEM((heads, tokens, width), f32)
        rows = pltpu.VMEM((tokens, total), f32)
        sems = pltpu.SemaphoreType.DMA((chunks,))
        return pl.pallas_call(
            functools.partial(kernel, n, per),
            out_shape=[jax.ShapeDtypeStruct((tokens, total), jnp.bfloat16)] * 4,
            in_specs=[pl.BlockSpec(memory_space=pltpu.HBM)] * 4 + [vmem],
            out_specs=[vmem] * 4,
            scratch_shapes=[pltpu.VMEM((tokens, total), jnp.bfloat16)] * 4
            + [state] * 4
            + [decay] * 3
            + [pltpu.VMEM((heads, 8, width), f32)]
            + [rows] * 4
            + [sems] * 4
            + [pltpu.SemaphoreType.DMA((4, GROUPS))],
            compiler_params=pltpu.CompilerParams(
                collective_id=0, has_side_effects=True, vmem_limit_bytes=48 * 1024 * 1024
            ),
        )(queries, key_vectors, values, out_grad, log_decay)

    spec = P(("dp", "ctx"), None)
    return jax.shard_map(
        shards, mesh=mesh, in_specs=(spec,) * 5, out_specs=(spec,) * 4, check_vma=False
    )
```
